32 devices in a mesh: link: 16 (over z, x, core), col: 2 (over y).
Axes of the slice: x: 2, y: 2, z: 4, core: 2. Of those that a mesh axis runs over, the one named last changes fastest.
Arguments:
- values: bfloat16 [256, 16, 128], P('link'), may hold values from -6 to 6
- tiles: int32 [256, 16], P('link'), may hold values from 0 to 31, all different within a row
- barrier: float32 [256], P('link'), may hold values from 0.5 to 2
- slack: float32 [4096], replicated, may hold values from 0.5 to 2
- order: int32 [32], replicated, may hold values from 0 to 31, each once
Outputs:
- factored: float32 [4096, 4096], P('link', 'col')
The draws below stay inside these ranges and needn't reach their ends.
Inputs may be any that keep to these rules, and one draw needn't show every extreme that they name: `tiles`: each commodity's 16 tile numbers are distinct, and every tile is named by some commodity. `order`: each tile number appears once.
All inputs are finite; a program needn't handle non-finite values.
Results may differ from the reference program's by a relative error of at most 0.0038.
Values may be sent and summed in bfloat16 or wider, within the bound.
A program may use at most 64 MiB of HBM per device.

```python
import jax
import jax.numpy as jnp
from jax import lax

TILE = 128
TPC = 16
PANEL = 128
K = 256
LINKS = 4096
LTILES = 32


def shard_levels(key, shape, split, smallest, largest):
    def one(axis_at, parts):
        draws = jax.random.uniform(jax.random.fold_in(jax.random.fold_in(key, 6), axis_at), (parts,), jnp.float32, smallest / len(split), largest / len(split))
        return jnp.repeat(jnp.exp(draws), shape[axis_at] // parts).reshape((-1,) + (1,) * (len(shape) - axis_at - 1))

    loudness = one(*split[0])
    for cut in split[1:]:
        loudness = loudness * one(*cut)
    return loudness


def different_ones(own_key, rows, number_of, top, lift):
    ranking = jax.random.permutation(jax.random.fold_in(own_key, 1), number_of)
    pull = ranking
    for power in range(3):
        pull = pull * pull // number_of
    pull = pull * lift // number_of
    tickets = jax.random.randint(jax.random.fold_in(own_key, 2), (rows, number_of), 0, 4096) + pull
    fixed_rows = jax.random.permutation(jax.random.fold_in(own_key, 3), rows)[jnp.arange(number_of) % rows]
    tickets = jnp.where(jnp.arange(rows)[:, None] == fixed_rows[None, :], 1 << 14, tickets)
    merit = tickets * number_of + jnp.arange(number_of)
    return lax.top_k(merit.astype(jnp.int32), top)[1].astype(jnp.int32)


def noise(own_key, dims, scale, limit, pieces=(), dtype=jnp.bfloat16):
    result = jax.random.normal(own_key, dims, jnp.float32) * scale
    if len(pieces) > 0:
        result = shard_levels(own_key, dims, pieces, -0.22, 0.18) * result
    return jnp.clip(result, min=-limit, max=limit).astype(dtype)


def setup_inputs(seed: int = 0) -> dict:
    splits = jax.random.split(jax.random.key(seed), 6)
    values = noise(splits[0], (K, TPC, TILE), 1.0, 6.0, ((0, 16),))
    tiles = different_ones(splits[1], K, LTILES, TPC, 0)
    barrier = jnp.clip(0.5 + 1.5 * jax.random.uniform(splits[2], (K,), jnp.float32) ** shard_levels(splits[2], (K,), ((0, 16),), -0.2, 0.2), 0.5, 2.0)
    slack = jnp.clip(jax.random.uniform(splits[3], (LINKS,), jnp.float32, 0.5, 2.0), 0.5, 2.0)
    order = jax.random.permutation(splits[4], LTILES).astype(jnp.int32)
    return {"values": values, "tiles": tiles, "barrier": barrier, "slack": slack, "order": order}


def reference(values, tiles, barrier, slack, order):
    factor = LINKS / (K * TPC * TILE)
    scaled = (jnp.sqrt(barrier * factor)[:, None, None] * values.astype(jnp.float32)).astype(jnp.bfloat16)
    onehot = (tiles[:, :, None] == order[None, None, :]).astype(jnp.float32)
    incidence = jnp.einsum('kjp,kju->kpu', onehot, scaled.astype(jnp.float32)).astype(jnp.bfloat16)
    incidence = incidence.reshape(K, LINKS)
    normal = jnp.dot(incidence.T.astype(jnp.float32), incidence.astype(jnp.float32), preferred_element_type=jnp.float32)
    slack_ord = slack.reshape(LTILES, TILE)[order].reshape(LINKS)
    diag_ids = jnp.arange(LINKS)
    matrix = normal.at[diag_ids, diag_ids].add(slack_ord)
    panels = []
    for panel_no in range(2):
        first_col = panel_no * PANEL
        lower_fac = jnp.linalg.cholesky(matrix[first_col:first_col + PANEL, first_col:first_col + PANEL])
        below_rows = matrix[first_col + PANEL:, first_col:first_col + PANEL]
        solved = jax.scipy.linalg.solve_triangular(lower_fac, below_rows.T, lower=True).T
        column = jnp.concatenate([jnp.zeros((first_col, PANEL), jnp.float32), lower_fac, solved], 0)
        rounded = column.astype(jnp.bfloat16)
        matrix = matrix - jnp.dot(rounded.astype(jnp.float32), rounded.T.astype(jnp.float32), preferred_element_type=jnp.float32)
        panels.append(column)
    rows_all = jnp.arange(LINKS)
    matrix = jnp.where(rows_all[:, None] < 2 * PANEL, jnp.float32(0.0), matrix)
    return matrix.at[:, :2 * PANEL].set(jnp.concatenate(panels, 1))
```

```python
import jax
import jax.numpy as jnp
from jax import lax
from jax.sharding import PartitionSpec as P

PANEL = 128


def contract_rows(left_side, right_side):
    return lax.dot_general(
        left_side, right_side, (((0,), (0,)), ((), ())), preferred_element_type=jnp.float32
    )


def local(values, tiles, barrier, slack, order):
    link_devs = lax.axis_size("link")
    col_devs = lax.axis_size("col")
    link_idx = lax.axis_index("link")
    col_idx = lax.axis_index("col")
    link_count = slack.shape[0]
    rows_dev = link_count // link_devs
    cols_dev = link_count // col_devs
    tpc, tile_len = values.shape[1:]
    ntiles = order.shape[0]
    head = 2 * PANEL
    factor = link_count / (values.shape[0] * link_devs * tpc * tile_len)
    scaled = (jnp.sqrt(barrier * factor)[:, None, None] * values.astype(jnp.float32)).astype(
        jnp.bfloat16
    )
    ids = jnp.pad(tiles.astype(jnp.bfloat16), ((0, 0), (0, tile_len - tpc)))
    packed = jnp.concatenate([scaled, ids[:, None, :]], 1)
    packed = lax.all_gather(packed, "link", axis=0, tiled=True)
    all_vals = packed[:, :tpc]
    all_ids = packed[:, tpc, :tpc].astype(jnp.int32)

    row_tiles = rows_dev // tile_len
    col_tiles = cols_dev // tile_len
    places = jnp.concatenate(
        [
            jnp.arange(head // tile_len),
            link_idx * row_tiles + jnp.arange(row_tiles),
            col_idx * col_tiles + jnp.arange(col_tiles),
        ]
    )
    place_hot = (places[:, None] == jnp.arange(ntiles)[None, :]).astype(jnp.int32)
    targets = jnp.sum(place_hot * order[None, :], 1)
    onehot = (all_ids[:, :, None] == targets[None, None, :]).astype(jnp.bfloat16)
    chosen = jnp.einsum("kjp,kju->kpu", onehot, all_vals, preferred_element_type=jnp.float32)
    chosen = chosen.astype(jnp.bfloat16).reshape(all_vals.shape[0], -1)
    cols_g = (places[:, None] * tile_len + jnp.arange(tile_len)[None, :]).reshape(-1)

    target_hot = (targets[: head // tile_len + row_tiles, None] == jnp.arange(ntiles)).astype(
        jnp.float32
    )
    slack_some = jnp.dot(
        target_hot, slack.reshape(ntiles, tile_len), precision=lax.Precision.HIGHEST
    ).reshape(-1)
    slack_head, slack_rows = slack_some[:head], slack_some[head:]

    panel_rows = jnp.arange(head)
    strip = contract_rows(chosen[:, :head], chosen)
    strip = strip + jnp.where(
        panel_rows[:, None] == cols_g[None, :], slack_head[:, None], jnp.float32(0.0)
    )
    keep = panel_rows[:, None] <= cols_g[None, :]
    done = []
    work = strip[:PANEL]
    for panel_no in range(2):
        first = panel_no * PANEL
        lower_fac = jnp.linalg.cholesky(work[:, first : first + PANEL])
        solved = jax.scipy.linalg.solve_triangular(lower_fac, work, lower=True)
        solved = jnp.where(keep[first : first + PANEL], solved, jnp.float32(0.0))
        done.append(solved)
        if panel_no == 0:
            rounded = solved.astype(jnp.bfloat16)
            work = strip[PANEL:] - contract_rows(rounded[:, PANEL:head], rounded)
    factors = jnp.concatenate(done, 0)
    rounded = factors.astype(jnp.bfloat16)
    mine = slice(head, head + rows_dev)
    left = jnp.concatenate([chosen[:, mine], -rounded[:, mine]], 0)
    right = jnp.concatenate([chosen[:, head + rows_dev :], rounded[:, head + rows_dev :]], 0)
    matrix = contract_rows(left, right)
    rows_g = cols_g[mine]
    out_g = cols_g[head + rows_dev :]
    matrix = matrix + jnp.where(
        rows_g[:, None] == out_g[None, :], slack_rows[:, None], jnp.float32(0.0)
    )
    padded = jnp.pad(factors[:, mine].T, ((0, 0), (0, cols_dev - head)))
    return jnp.where(
        out_g[None, :] < head,
        padded,
        jnp.where(rows_g[:, None] < head, jnp.float32(0.0), matrix),
    )


def solution(mesh):
    in_specs = (P("link", None, None), P("link", None), P("link"), P(), P())
    out_specs = P("link", "col")
    return jax.shard_map(local, mesh=mesh, in_specs=in_specs, out_specs=out_specs, check_vma=False)
```

```python
import jax
import jax.numpy as jnp
from jax import lax
from jax.experimental import pallas as pl
from jax.experimental.pallas import tpu as pltpu
from jax.sharding import PartitionSpec as P

PANEL = 128
STEP = 4


def contract_rows(left_side, right_side):
    return lax.dot_general(
        left_side, right_side, (((0,), (0,)), ((), ())), preferred_element_type=jnp.float32
    )


def inverse_kernel(block_ref, out_ref):
    size = PANEL
    row_ids = lax.broadcasted_iota(jnp.int32, (size, size), 0)
    col_ids = lax.broadcasted_iota(jnp.int32, (size, size), 1)
    left = block_ref[...]
    right = (row_ids == col_ids).astype(jnp.float32)
    for first in range(0, size, STEP):
        inner = first % 8
        if inner == 0 and first > 0:
            left, right = left[8:], right[8:]
        lefts = [left[inner + t : inner + t + 1] for t in range(STEP)]
        rights = [right[inner + t : inner + t + 1] for t in range(STEP)]
        small = {
            (t, s): jnp.broadcast_to(lefts[t][:, first + s : first + s + 1], (1, size))
            for t in range(STEP)
            for s in range(t, STEP)
        }
        ratio, flipped = {}, []
        for t in range(STEP):
            flipped.append(1.0 / small[t, t])
            for s in range(t + 1, STEP):
                ratio[t, s] = small[t, s] * flipped[t]
                for u in range(s, STEP):
                    small[s, u] = small[s, u] - ratio[t, s] * small[t, u]
                lefts[s] = lefts[s] - ratio[t, s] * lefts[t]
                rights[s] = rights[s] - ratio[t, s] * rights[t]
        for t in range(STEP):
            out_ref[first + t : first + t + 1, :] = rights[t] * lax.rsqrt(small[t, t])
        if first + STEP == size:
            break
        lefts = [lefts[t] * flipped[t] for t in range(STEP)]
        rights = [rights[t] * flipped[t] for t in range(STEP)]
        for t in range(STEP - 2, -1, -1):
            for s in range(t + 1, STEP):
                lefts[t] = lefts[t] - ratio[t, s] * lefts[s]
                rights[t] = rights[t] - ratio[t, s] * rights[s]
        spread = [
            jnp.broadcast_to(left[:, first + t : first + t + 1], left.shape) for t in range(STEP)
        ]
        for t in range(STEP):
            left = left - spread[t] * lefts[t]
            right = right - spread[t] * rights[t]


def inverse_factor(block):
    return pl.pallas_call(
        inverse_kernel,
        out_shape=jax.ShapeDtypeStruct((PANEL, PANEL), jnp.float32),
        in_specs=[pl.BlockSpec(memory_space=pltpu.VMEM)],
        out_specs=pl.BlockSpec(memory_space=pltpu.VMEM),
    )(block)


def local(values, tiles, barrier, slack, order):
    link_devs = lax.axis_size("link")
    col_devs = lax.axis_size("col")
    link_idx = lax.axis_index("link")
    col_idx = lax.axis_index("col")
    link_count = slack.shape[0]
    rows_dev = link_count // link_devs
    cols_dev = link_count // col_devs
    tpc, tile_len = values.shape[1:]
    ntiles = order.shape[0]
    head = 2 * PANEL
    factor = link_count / (values.shape[0] * link_devs * tpc * tile_len)
    scaled = (jnp.sqrt(barrier * factor)[:, None, None] * values.astype(jnp.float32)).astype(
        jnp.bfloat16
    )
    ids = jnp.pad(tiles.astype(jnp.bfloat16), ((0, 0), (0, tile_len - tpc)))
    packed = jnp.concatenate([scaled, ids[:, None, :]], 1)
    packed = lax.all_gather(packed, "link", axis=0, tiled=True)
    all_vals = packed[:, :tpc]
    all_ids = packed[:, tpc, :tpc].astype(jnp.int32)

    row_tiles = rows_dev // tile_len
    col_tiles = cols_dev // tile_len
    places = jnp.concatenate(
        [
            jnp.arange(head // tile_len),
            link_idx * row_tiles + jnp.arange(row_tiles),
            col_idx * col_tiles + jnp.arange(col_tiles),
        ]
    )
    place_hot = (places[:, None] == jnp.arange(ntiles)[None, :]).astype(jnp.int32)
    targets = jnp.sum(place_hot * order[None, :], 1)
    onehot = (all_ids[:, :, None] == targets[None, None, :]).astype(jnp.bfloat16)
    chosen = jnp.einsum("kjp,kju->kpu", onehot, all_vals, preferred_element_type=jnp.float32)
    chosen = chosen.astype(jnp.bfloat16).reshape(all_vals.shape[0], -1)
    cols_g = (places[:, None] * tile_len + jnp.arange(tile_len)[None, :]).reshape(-1)

    target_hot = (targets[: head // tile_len + row_tiles, None] == jnp.arange(ntiles)).astype(
        jnp.float32
    )
    slack_some = jnp.dot(
        target_hot, slack.reshape(ntiles, tile_len), precision=lax.Precision.HIGHEST
    ).reshape(-1)
    slack_head, slack_rows = slack_some[:head], slack_some[head:]

    panel_rows = jnp.arange(head)
    strip = contract_rows(chosen[:, :head], chosen)
    strip = strip + jnp.where(
        panel_rows[:, None] == cols_g[None, :], slack_head[:, None], jnp.float32(0.0)
    )
    keep = panel_rows[:, None] <= cols_g[None, :]
    done = []
    work = strip[:PANEL]
    for panel_no in range(2):
        first = panel_no * PANEL
        lower_inv = inverse_factor(work[:, first : first + PANEL])
        solved = jnp.dot(lower_inv, work, precision=lax.Precision.HIGHEST)
        solved = jnp.where(keep[first : first + PANEL], solved, jnp.float32(0.0))
        done.append(solved)
        if panel_no == 0:
            rounded = solved.astype(jnp.bfloat16)
            work = strip[PANEL:] - contract_rows(rounded[:, PANEL:head], rounded)
    factors = jnp.concatenate(done, 0)
    rounded = factors.astype(jnp.bfloat16)
    mine = slice(head, head + rows_dev)
    left = jnp.concatenate([chosen[:, mine], -rounded[:, mine]], 0)
    right = jnp.concatenate([chosen[:, head + rows_dev :], rounded[:, head + rows_dev :]], 0)
    matrix = contract_rows(left, right)
    rows_g = cols_g[mine]
    out_g = cols_g[head + rows_dev :]
    matrix = matrix + jnp.where(
        rows_g[:, None] == out_g[None, :], slack_rows[:, None], jnp.float32(0.0)
    )
    padded = jnp.pad(factors[:, mine].T, ((0, 0), (0, cols_dev - head)))
    return jnp.where(
        out_g[None, :] < head,
        padded,
        jnp.where(rows_g[:, None] < head, jnp.float32(0.0), matrix),
    )


def solution(mesh):
    in_specs = (P("link", None, None), P("link", None), P("link"), P(), P())
    out_specs = P("link", "col")
    return jax.shard_map(local, mesh=mesh, in_specs=in_specs, out_specs=out_specs, check_vma=False)
```

```python
import functools

import jax
import jax.numpy as jnp
from jax import lax
from jax.experimental import pallas as pl
from jax.experimental.pallas import tpu as pltpu
from jax.sharding import PartitionSpec as P

PANEL = 128
STEP = 4


def contract_rows(left_side, right_side):
    return lax.dot_general(
        left_side, right_side, (((0,), (0,)), ((), ())), preferred_element_type=jnp.float32
    )


def inverse_kernel(block_ref, out_ref):
    size = PANEL
    row_ids = lax.broadcasted_iota(jnp.int32, (size, size), 0)
    col_ids = lax.broadcasted_iota(jnp.int32, (size, size), 1)
    left = block_ref[...]
    right = (row_ids == col_ids).astype(jnp.float32)
    for first in range(0, size, STEP):
        inner = first % 8
        if inner == 0 and first > 0:
            left, right = left[8:], right[8:]
        lefts = [left[inner + t : inner + t + 1] for t in range(STEP)]
        rights = [right[inner + t : inner + t + 1] for t in range(STEP)]
        small = {
            (t, s): jnp.broadcast_to(lefts[t][:, first + s : first + s + 1], (1, size))
            for t in range(STEP)
            for s in range(t, STEP)
        }
        ratio, flipped = {}, []
        for t in range(STEP):
            flipped.append(1.0 / small[t, t])
            for s in range(t + 1, STEP):
                ratio[t, s] = small[t, s] * flipped[t]
                for u in range(s, STEP):
                    small[s, u] = small[s, u] - ratio[t, s] * small[t, u]
                lefts[s] = lefts[s] - ratio[t, s] * lefts[t]
                rights[s] = rights[s] - ratio[t, s] * rights[t]
        for t in range(STEP):
            out_ref[first + t : first + t + 1, :] = rights[t] * lax.rsqrt(small[t, t])
        if first + STEP == size:
            break
        lefts = [lefts[t] * flipped[t] for t in range(STEP)]
        rights = [rights[t] * flipped[t] for t in range(STEP)]
        for t in range(STEP - 2, -1, -1):
            for s in range(t + 1, STEP):
                lefts[t] = lefts[t] - ratio[t, s] * lefts[s]
                rights[t] = rights[t] - ratio[t, s] * rights[s]
        spread = [
            jnp.broadcast_to(left[:, first + t : first + t + 1], left.shape) for t in range(STEP)
        ]
        for t in range(STEP):
            left = left - spread[t] * lefts[t]
            right = right - spread[t] * rights[t]


def inverse_factor(block):
    return pl.pallas_call(
        inverse_kernel,
        out_shape=jax.ShapeDtypeStruct((PANEL, PANEL), jnp.float32),
        in_specs=[pl.BlockSpec(memory_space=pltpu.VMEM)],
        out_specs=pl.BlockSpec(memory_space=pltpu.VMEM),
    )(block)


def gather_kernel(n, own_ref, out_ref, send_sem, pass_sem, recv_sem):
    me = lax.axis_index("link")
    core = me % 2
    other = me + 1 - 2 * core
    chip = me // 2
    chips = n // 2
    peers = [((chip + step) % chips) * 2 + core for step in range(1, chips)]
    barrier = pltpu.get_barrier_semaphore()
    for peer in peers + [other]:
        pl.semaphore_signal(
            barrier, inc=1, device_id={"link": peer}, device_id_type=pl.DeviceIdType.MESH
        )
    pl.semaphore_wait(barrier, chips)

    def move(src, owner, send, target):
        return pltpu.make_async_remote_copy(
            src_ref=src,
            dst_ref=out_ref.at[owner],
            send_sem=send,
            recv_sem=recv_sem.at[owner],
            device_id={"link": target},
            device_id_type=pl.DeviceIdType.MESH,
        )

    sent = [move(own_ref, me, send_sem.at[i], peer) for i, peer in enumerate(peers + [other])]
    for copy in sent:
        copy.start()
    out_ref[me] = own_ref[...]
    passed = []
    for step in range(1, chips):
        owner = ((chip + chips - step) % chips) * 2 + core
        copy = move(out_ref.at[owner], owner, pass_sem.at[step], other)
        copy.wait_recv()
        copy.start()
        passed.append(copy)
    for step in range(chips):
        owner = ((chip + chips - step) % chips) * 2 + 1 - core
        move(own_ref, owner, send_sem.at[0], other).wait_recv()
    for copy in sent + passed:
        copy.wait_send()


def gather_blocks(own, n):
    return pl.pallas_call(
        functools.partial(gather_kernel, n),
        out_shape=jax.ShapeDtypeStruct((n,) + own.shape, own.dtype),
        in_specs=[pl.BlockSpec(memory_space=pltpu.VMEM)],
        out_specs=pl.BlockSpec(memory_space=pltpu.VMEM),
        scratch_shapes=[
            pltpu.SemaphoreType.DMA((n // 2,)),
            pltpu.SemaphoreType.DMA((n // 2,)),
            pltpu.SemaphoreType.DMA((n,)),
        ],
        compiler_params=pltpu.CompilerParams(collective_id=0, has_side_effects=True),
    )(own)


def local(values, tiles, barrier, slack, order):
    link_devs = lax.axis_size("link")
    col_devs = lax.axis_size("col")
    link_idx = lax.axis_index("link")
    col_idx = lax.axis_index("col")
    link_count = slack.shape[0]
    rows_dev = link_count // link_devs
    cols_dev = link_count // col_devs
    tpc, tile_len = values.shape[1:]
    ntiles = order.shape[0]
    head = 2 * PANEL
    factor = link_count / (values.shape[0] * link_devs * tpc * tile_len)
    scaled = (jnp.sqrt(barrier * factor)[:, None, None] * values.astype(jnp.float32)).astype(
        jnp.bfloat16
    )
    ids = jnp.pad(tiles.astype(jnp.bfloat16), ((0, 0), (0, tile_len - tpc)))
    per_dev = values.shape[0]
    packed = jnp.concatenate([scaled.reshape(per_dev * tpc, tile_len), ids], 0)
    packed = gather_blocks(packed, link_devs)
    all_vals = packed[:, : per_dev * tpc].reshape(-1, tpc, tile_len)
    all_ids = packed[:, per_dev * tpc :, :tpc].astype(jnp.int32).reshape(-1, tpc)

    row_tiles = rows_dev // tile_len
    col_tiles = cols_dev // tile_len
    places = jnp.concatenate(
        [
            jnp.arange(head // tile_len),
            link_idx * row_tiles + jnp.arange(row_tiles),
            col_idx * col_tiles + jnp.arange(col_tiles),
        ]
    )
    place_hot = (places[:, None] == jnp.arange(ntiles)[None, :]).astype(jnp.int32)
    targets = jnp.sum(place_hot * order[None, :], 1)
    onehot = (all_ids[:, :, None] == targets[None, None, :]).astype(jnp.bfloat16)
    chosen = jnp.einsum("kjp,kju->kpu", onehot, all_vals, preferred_element_type=jnp.float32)
    chosen = chosen.astype(jnp.bfloat16).reshape(all_vals.shape[0], -1)
    cols_g = (places[:, None] * tile_len + jnp.arange(tile_len)[None, :]).reshape(-1)

    target_hot = (targets[: head // tile_len + row_tiles, None] == jnp.arange(ntiles)).astype(
        jnp.float32
    )
    slack_some = jnp.dot(
        target_hot, slack.reshape(ntiles, tile_len), precision=lax.Precision.HIGHEST
    ).reshape(-1)
    slack_head, slack_rows = slack_some[:head], slack_some[head:]

    panel_rows = jnp.arange(head)
    strip = contract_rows(chosen[:, :head], chosen)
    strip = strip + jnp.where(
        panel_rows[:, None] == cols_g[None, :], slack_head[:, None], jnp.float32(0.0)
    )
    keep = panel_rows[:, None] <= cols_g[None, :]
    done = []
    work = strip[:PANEL]
    for panel_no in range(2):
        first = panel_no * PANEL
        lower_inv = inverse_factor(work[:, first : first + PANEL])
        solved = jnp.dot(lower_inv, work, precision=lax.Precision.HIGHEST)
        solved = jnp.where(keep[first : first + PANEL], solved, jnp.float32(0.0))
        done.append(solved)
        if panel_no == 0:
            rounded = solved.astype(jnp.bfloat16)
            work = strip[PANEL:] - contract_rows(rounded[:, PANEL:head], rounded)
    factors = jnp.concatenate(done, 0)
    rounded = factors.astype(jnp.bfloat16)
    mine = slice(head, head + rows_dev)
    left = jnp.concatenate([chosen[:, mine], -rounded[:, mine]], 0)
    right = jnp.concatenate([chosen[:, head + rows_dev :], rounded[:, head + rows_dev :]], 0)
    matrix = contract_rows(left, right)
    rows_g = cols_g[mine]
    out_g = cols_g[head + rows_dev :]
    matrix = matrix + jnp.where(
        rows_g[:, None] == out_g[None, :], slack_rows[:, None], jnp.float32(0.0)
    )
    padded = jnp.pad(factors[:, mine].T, ((0, 0), (0, cols_dev - head)))
    return jnp.where(
        out_g[None, :] < head,
        padded,
        jnp.where(rows_g[:, None] < head, jnp.float32(0.0), matrix),
    )


def solution(mesh):
    in_specs = (P("link", None, None), P("link", None), P("link"), P(), P())
    out_specs = P("link", "col")
    return jax.shard_map(local, mesh=mesh, in_specs=in_specs, out_specs=out_specs, check_vma=False)
```

```python
import functools

import jax
import jax.numpy as jnp
from jax import lax
from jax.experimental import pallas as pl
from jax.experimental.pallas import tpu as pltpu
from jax.sharding import PartitionSpec as P

PANEL = 128
STEP = 8


def contract_rows(left_side, right_side):
    return lax.dot_general(
        left_side, right_side, (((0,), (0,)), ((), ())), preferred_element_type=jnp.float32
    )


def inverse_kernel(block_ref, out_ref):
    size = PANEL
    row_ids = lax.broadcasted_iota(jnp.int32, (size, size), 0)
    col_ids = lax.broadcasted_iota(jnp.int32, (size, size), 1)
    left = block_ref[...]
    right = (row_ids == col_ids).astype(jnp.float32)
    for first in range(0, size, STEP):
        inner = first % 8
        if inner == 0 and first > 0:
            left, right = left[8:], right[8:]
        lefts = [left[inner + t : inner + t + 1] for t in range(STEP)]
        rights = [right[inner + t : inner + t + 1] for t in range(STEP)]
        small = {
            (t, s): jnp.broadcast_to(lefts[t][:, first + s : first + s + 1], (1, size))
            for t in range(STEP)
            for s in range(t, STEP)
        }
        ratio, flipped = {}, []
        for t in range(STEP):
            flipped.append(1.0 / small[t, t])
            for s in range(t + 1, STEP):
                ratio[t, s] = small[t, s] * flipped[t]
                for u in range(s, STEP):
                    small[s, u] = small[s, u] - ratio[t, s] * small[t, u]
                lefts[s] = lefts[s] - ratio[t, s] * lefts[t]
                rights[s] = rights[s] - ratio[t, s] * rights[t]
        for t in range(STEP):
            out_ref[first + t : first + t + 1, :] = rights[t] * lax.rsqrt(small[t, t])
        if first + STEP == size:
            break
        lefts = [lefts[t] * flipped[t] for t in range(STEP)]
        rights = [rights[t] * flipped[t] for t in range(STEP)]
        for t in range(STEP - 2, -1, -1):
            for s in range(t + 1, STEP):
                lefts[t] = lefts[t] - ratio[t, s] * lefts[s]
                rights[t] = rights[t] - ratio[t, s] * rights[s]
        spread = [
            jnp.broadcast_to(left[:, first + t : first + t + 1], left.shape) for t in range(STEP)
        ]
        for t in range(STEP):
            left = left - spread[t] * lefts[t]
            right = right - spread[t] * rights[t]


def inverse_factor(block):
    return pl.pallas_call(
        inverse_kernel,
        out_shape=jax.ShapeDtypeStruct((PANEL, PANEL), jnp.float32),
        in_specs=[pl.BlockSpec(memory_space=pltpu.VMEM)],
        out_specs=pl.BlockSpec(memory_space=pltpu.VMEM),
    )(block)


def gather_kernel(n, own_ref, out_ref, send_sem, pass_sem, recv_sem):
    me = lax.axis_index("link")
    core = me % 2
    other = me + 1 - 2 * core
    chip = me // 2
    chips = n // 2
    peers = [((chip + step) % chips) * 2 + core for step in range(1, chips)]
    barrier = pltpu.get_barrier_semaphore()
    for peer in peers + [other]:
        pl.semaphore_signal(
            barrier, inc=1, device_id={"link": peer}, device_id_type=pl.DeviceIdType.MESH
        )
    pl.semaphore_wait(barrier, chips)

    def move(src, owner, send, target):
        return pltpu.make_async_remote_copy(
            src_ref=src,
            dst_ref=out_ref.at[owner],
            send_sem=send,
            recv_sem=recv_sem.at[owner],
            device_id={"link": target},
            device_id_type=pl.DeviceIdType.MESH,
        )

    sent = [move(own_ref, me, send_sem.at[i], peer) for i, peer in enumerate(peers + [other])]
    for copy in sent:
        copy.start()
    out_ref[me] = own_ref[...]
    passed = []
    for step in range(1, chips):
        owner = ((chip + chips - step) % chips) * 2 + core
        copy = move(out_ref.at[owner], owner, pass_sem.at[step], other)
        copy.wait_recv()
        copy.start()
        passed.append(copy)
    for step in range(chips):
        owner = ((chip + chips - step) % chips) * 2 + 1 - core
        move(own_ref, owner, send_sem.at[0], other).wait_recv()
    for copy in sent + passed:
        copy.wait_send()


def gather_blocks(own, n):
    return pl.pallas_call(
        functools.partial(gather_kernel, n),
        out_shape=jax.ShapeDtypeStruct((n,) + own.shape, own.dtype),
        in_specs=[pl.BlockSpec(memory_space=pltpu.VMEM)],
        out_specs=pl.BlockSpec(memory_space=pltpu.VMEM),
        scratch_shapes=[
            pltpu.SemaphoreType.DMA((n // 2,)),
            pltpu.SemaphoreType.DMA((n // 2,)),
            pltpu.SemaphoreType.DMA((n,)),
        ],
        compiler_params=pltpu.CompilerParams(collective_id=0, has_side_effects=True),
    )(own)


def local(values, tiles, barrier, slack, order):
    link_devs = lax.axis_size("link")
    col_devs = lax.axis_size("col")
    link_idx = lax.axis_index("link")
    col_idx = lax.axis_index("col")
    link_count = slack.shape[0]
    rows_dev = link_count // link_devs
    cols_dev = link_count // col_devs
    tpc, tile_len = values.shape[1:]
    ntiles = order.shape[0]
    head = 2 * PANEL
    factor = link_count / (values.shape[0] * link_devs * tpc * tile_len)
    scaled = (jnp.sqrt(barrier * factor)[:, None, None] * values.astype(jnp.float32)).astype(
        jnp.bfloat16
    )
    ids = jnp.pad(tiles.astype(jnp.bfloat16), ((0, 0), (0, tile_len - tpc)))
    per_dev = values.shape[0]
    packed = jnp.concatenate([scaled.reshape(per_dev * tpc, tile_len), ids], 0)
    packed = gather_blocks(packed, link_devs)
    all_vals = packed[:, : per_dev * tpc].reshape(-1, tpc, tile_len)
    all_ids = packed[:, per_dev * tpc :, :tpc].astype(jnp.int32).reshape(-1, tpc)

    row_tiles = rows_dev // tile_len
    col_tiles = cols_dev // tile_len
    places = jnp.concatenate(
        [
            jnp.arange(head // tile_len),
            link_idx * row_tiles + jnp.arange(row_tiles),
            col_idx * col_tiles + jnp.arange(col_tiles),
        ]
    )
    place_hot = (places[:, None] == jnp.arange(ntiles)[None, :]).astype(jnp.int32)
    targets = jnp.sum(place_hot * order[None, :], 1)
    onehot = (all_ids[:, :, None] == targets[None, None, :]).astype(jnp.bfloat16)
    chosen = jnp.einsum("kjp,kju->kpu", onehot, all_vals, preferred_element_type=jnp.float32)
    chosen = chosen.astype(jnp.bfloat16).reshape(all_vals.shape[0], -1)
    cols_g = (places[:, None] * tile_len + jnp.arange(tile_len)[None, :]).reshape(-1)

    target_hot = targets[: head // tile_len + row_tiles, None] == jnp.arange(ntiles)[None, :]
    slack_some = jnp.sum(
        jnp.where(target_hot[:, :, None], slack.reshape(1, ntiles, tile_len), jnp.float32(0.0)), 1
    ).reshape(-1)
    slack_head, slack_rows = slack_some[:head], slack_some[head:]

    panel_rows = jnp.arange(head)
    strip = contract_rows(chosen[:, :head], chosen)
    strip = strip + jnp.where(
        panel_rows[:, None] == cols_g[None, :], slack_head[:, None], jnp.float32(0.0)
    )
    keep = panel_rows[:, None] <= cols_g[None, :]
    done = []
    work = strip[:PANEL]
    for panel_no in range(2):
        first = panel_no * PANEL
        lower_inv = inverse_factor(work[:, first : first + PANEL])
        solved = jnp.dot(lower_inv, work, precision=lax.Precision.HIGHEST)
        solved = jnp.where(keep[first : first + PANEL], solved, jnp.float32(0.0))
        done.append(solved)
        if panel_no == 0:
            rounded = solved.astype(jnp.bfloat16)
            work = strip[PANEL:] - contract_rows(rounded[:, PANEL:head], rounded)
    factors = jnp.concatenate(done, 0)
    rounded = factors.astype(jnp.bfloat16)
    mine = slice(head, head + rows_dev)
    left = jnp.concatenate([chosen[:, mine], -rounded[:, mine]], 0)
    right = jnp.concatenate([chosen[:, head + rows_dev :], rounded[:, head + rows_dev :]], 0)
    matrix = contract_rows(left, right)
    rows_g = cols_g[mine]
    out_g = cols_g[head + rows_dev :]
    matrix = matrix + jnp.where(
        rows_g[:, None] == out_g[None, :], slack_rows[:, None], jnp.float32(0.0)
    )
    padded = jnp.pad(factors[:, mine].T, ((0, 0), (0, cols_dev - head)))
    return jnp.where(
        out_g[None, :] < head,
        padded,
        jnp.where(rows_g[:, None] < head, jnp.float32(0.0), matrix),
    )


def solution(mesh):
    in_specs = (P("link", None, None), P("link", None), P("link"), P(), P())
    out_specs = P("link", "col")
    return jax.shard_map(local, mesh=mesh, in_specs=in_specs, out_specs=out_specs, check_vma=False)
```

```python
import functools

import jax
import jax.numpy as jnp
from jax import lax
from jax.experimental import pallas as pl
from jax.experimental.pallas import tpu as pltpu
from jax.sharding import PartitionSpec as P

PANEL = 128
STEP = 8


def contract_rows(left_side, right_side):
    return lax.dot_general(
        left_side, right_side, (((0,), (0,)), ((), ())), preferred_element_type=jnp.float32
    )


def inverse_kernel(block_ref, out_ref):
    size = PANEL
    row_ids = lax.broadcasted_iota(jnp.int32, (size, size), 0)
    col_ids = lax.broadcasted_iota(jnp.int32, (size, size), 1)
    left = block_ref[...]
    right = (row_ids == col_ids).astype(jnp.float32)
    for first in range(0, size, STEP):
        inner = first % 8
        if inner == 0 and first > 0:
            left, right = left[8:], right[8:]
        lefts = [left[inner + t : inner + t + 1] for t in range(STEP)]
        rights = [right[inner + t : inner + t + 1] for t in range(STEP)]
        small = {
            (t, s): jnp.broadcast_to(lefts[t][:, first + s : first + s + 1], (1, size))
            for t in range(STEP)
            for s in range(t, STEP)
        }
        ratio, flipped = {}, []
        for t in range(STEP):
            flipped.append(1.0 / small[t, t])
            for s in range(t + 1, STEP):
                ratio[t, s] = small[t, s] * flipped[t]
                for u in range(s, STEP):
                    small[s, u] = small[s, u] - ratio[t, s] * small[t, u]
                lefts[s] = lefts[s] - ratio[t, s] * lefts[t]
                rights[s] = rights[s] - ratio[t, s] * rights[t]
        for t in range(STEP):
            out_ref[first + t : first + t + 1, :] = rights[t] * lax.rsqrt(small[t, t])
        if first + STEP == size:
            break
        lefts = [lefts[t] * flipped[t] for t in range(STEP)]
        rights = [rights[t] * flipped[t] for t in range(STEP)]
        for t in range(STEP - 2, -1, -1):
            for s in range(t + 1, STEP):
                lefts[t] = lefts[t] - ratio[t, s] * lefts[s]
                rights[t] = rights[t] - ratio[t, s] * rights[s]
        spread = [
            jnp.broadcast_to(left[:, first + t : first + t + 1], left.shape) for t in range(STEP)
        ]
        for t in range(STEP):
            left = left - spread[t] * lefts[t]
            right = right - spread[t] * rights[t]


def inverse_factor(block):
    return pl.pallas_call(
        inverse_kernel,
        out_shape=jax.ShapeDtypeStruct((PANEL, PANEL), jnp.float32),
        in_specs=[pl.BlockSpec(memory_space=pltpu.VMEM)],
        out_specs=pl.BlockSpec(memory_space=pltpu.VMEM),
    )(block)


def gather_kernel(n, own_ref, out_ref, send_sem, pass_sem, recv_sem):
    me = lax.axis_index("link")
    core = me % 2
    other = me + 1 - 2 * core
    chip = me // 2
    chips = n // 2
    peers = [((chip + step) % chips) * 2 + core for step in range(1, chips)]
    barrier = pltpu.get_barrier_semaphore()
    for peer in peers + [other]:
        pl.semaphore_signal(
            barrier, inc=1, device_id={"link": peer}, device_id_type=pl.DeviceIdType.MESH
        )
    pl.semaphore_wait(barrier, chips)

    def move(src, owner, send, target):
        return pltpu.make_async_remote_copy(
            src_ref=src,
            dst_ref=out_ref.at[owner],
            send_sem=send,
            recv_sem=recv_sem.at[owner],
            device_id={"link": target},
            device_id_type=pl.DeviceIdType.MESH,
        )

    sent = [move(own_ref, me, send_sem.at[i], peer) for i, peer in enumerate(peers + [other])]
    for copy in sent:
        copy.start()
    out_ref[me] = own_ref[...]
    passed = []
    for step in range(1, chips):
        owner = ((chip + chips - step) % chips) * 2 + core
        copy = move(out_ref.at[owner], owner, pass_sem.at[step], other)
        copy.wait_recv()
        copy.start()
        passed.append(copy)
    for step in range(chips):
        owner = ((chip + chips - step) % chips) * 2 + 1 - core
        move(own_ref, owner, send_sem.at[0], other).wait_recv()
    for copy in sent + passed:
        copy.wait_send()


def gather_blocks(own, n):
    return pl.pallas_call(
        functools.partial(gather_kernel, n),
        out_shape=jax.ShapeDtypeStruct((n,) + own.shape, own.dtype),
        in_specs=[pl.BlockSpec(memory_space=pltpu.VMEM)],
        out_specs=pl.BlockSpec(memory_space=pltpu.VMEM),
        scratch_shapes=[
            pltpu.SemaphoreType.DMA((n // 2,)),
            pltpu.SemaphoreType.DMA((n // 2,)),
            pltpu.SemaphoreType.DMA((n,)),
        ],
        compiler_params=pltpu.CompilerParams(collective_id=0, has_side_effects=True),
    )(own)


def local(values, tiles, barrier, slack, order):
    link_devs = lax.axis_size("link")
    col_devs = lax.axis_size("col")
    link_idx = lax.axis_index("link")
    col_idx = lax.axis_index("col")
    link_count = slack.shape[0]
    rows_dev = link_count // link_devs
    cols_dev = link_count // col_devs
    tpc, tile_len = values.shape[1:]
    ntiles = order.shape[0]
    head = 2 * PANEL
    factor = link_count / (values.shape[0] * link_devs * tpc * tile_len)
    scaled = (jnp.sqrt(barrier * factor)[:, None, None] * values.astype(jnp.float32)).astype(
        jnp.bfloat16
    )
    ids = jnp.pad(tiles.astype(jnp.bfloat16), ((0, 0), (0, tile_len - tpc)))
    per_dev = values.shape[0]
    packed = jnp.concatenate([scaled.reshape(per_dev * tpc, tile_len), ids], 0)
    packed = gather_blocks(packed, link_devs)
    all_vals = packed[:, : per_dev * tpc].reshape(-1, tpc, tile_len)
    all_ids = packed[:, per_dev * tpc :, :tpc].astype(jnp.int32).reshape(-1, tpc)

    row_tiles = rows_dev // tile_len
    col_tiles = cols_dev // tile_len
    places = jnp.concatenate(
        [
            jnp.arange(head // tile_len),
            link_idx * row_tiles + jnp.arange(row_tiles),
            col_idx * col_tiles + jnp.arange(col_tiles),
        ]
    )
    place_hot = (places[:, None] == jnp.arange(ntiles)[None, :]).astype(jnp.int32)
    targets = jnp.sum(place_hot * order[None, :], 1)
    onehot = (all_ids[:, :, None] == targets[None, None, :]).astype(jnp.bfloat16)
    chosen = jnp.einsum("kjp,kju->kpu", onehot, all_vals, preferred_element_type=jnp.float32)
    chosen = chosen.astype(jnp.bfloat16).reshape(all_vals.shape[0], -1)
    rows_g = link_idx * rows_dev + jnp.arange(rows_dev)
    out_g = col_idx * cols_dev + jnp.arange(cols_dev)
    at = jnp.arange(head + rows_dev + cols_dev)
    cols_g = jnp.where(
        at < head,
        at,
        jnp.where(
            at < head + rows_dev,
            at + (link_idx * rows_dev - head),
            at + (col_idx * cols_dev - head - rows_dev),
        ),
    )

    target_hot = targets[: head // tile_len + row_tiles, None] == jnp.arange(ntiles)[None, :]
    slack_some = jnp.sum(
        jnp.where(target_hot[:, :, None], slack.reshape(1, ntiles, tile_len), jnp.float32(0.0)), 1
    ).reshape(-1)
    slack_head, slack_rows = slack_some[:head], slack_some[head:]

    panel_rows = jnp.arange(head)
    strip = contract_rows(chosen[:, :head], chosen)
    strip = strip + jnp.where(
        panel_rows[:, None] == cols_g[None, :], slack_head[:, None], jnp.float32(0.0)
    )
    keep = panel_rows[:, None] <= cols_g[None, :]
    done = []
    work = strip[:PANEL]
    for panel_no in range(2):
        first = panel_no * PANEL
        lower_inv = inverse_factor(work[:, first : first + PANEL])
        solved = jnp.dot(lower_inv, work, precision=lax.Precision.HIGHEST)
        solved = jnp.where(keep[first : first + PANEL], solved, jnp.float32(0.0))
        done.append(solved)
        if panel_no == 0:
            rounded = solved.astype(jnp.bfloat16)
            work = strip[PANEL:] - contract_rows(rounded[:, PANEL:head], rounded)
    factors = jnp.concatenate(done, 0)
    rounded = factors.astype(jnp.bfloat16)
    mine = slice(head, head + rows_dev)
    left = jnp.concatenate([chosen[:, mine], -rounded[:, mine]], 0)
    right = jnp.concatenate([chosen[:, head + rows_dev :], rounded[:, head + rows_dev :]], 0)
    matrix = contract_rows(left, right)
    matrix = matrix + jnp.where(
        rows_g[:, None] == out_g[None, :], slack_rows[:, None], jnp.float32(0.0)
    )
    padded = jnp.pad(factors[:, mine].T, ((0, 0), (0, cols_dev - head)))
    return jnp.where(
        out_g[None, :] < head,
        padded,
        jnp.where(rows_g[:, None] < head, jnp.float32(0.0), matrix),
    )


def solution(mesh):
    in_specs = (P("link", None, None), P("link", None), P("link"), P(), P())
    out_specs = P("link", "col")
    return jax.shard_map(local, mesh=mesh, in_specs=in_specs, out_specs=out_specs, check_vma=False)
```
